1024 devices in a mesh: dp: 128 (over z, x, core), tensor: 8 (over y).
Axes of the slice: x: 8, y: 8, z: 8, core: 2. Of those that a mesh axis runs over, the one named last changes fastest.
Arguments:
- saved_x: bfloat16 [65536, 5120], P('dp', 'tensor'), may hold values from -6 to 6
- grad_key: bfloat16 [65536, 1024], P('dp', 'tensor'), may hold values from -24 to 24
- w_key: bfloat16 [1024, 5120], P('dp', 'tensor'), may hold values from -0.1875 to 0.1875
- lengths: int32 [128], replicated, may hold values from 128 to 512, as said below
Outputs:
- grad_input: bfloat16 [65536, 5120], P('dp', 'tensor')
- grad_weight: float32 [1024, 5120], P('dp', 'tensor')
The draws below stay inside these ranges and needn't reach their ends.
Inputs may be any that keep to these rules, and one draw needn't show every extreme that they name: `lengths`: each is a multiple of 128; group 0 is full and group 1 holds one block.
All inputs are finite; a program needn't handle non-finite values.
Results may differ from the reference program's by a relative error of at most 0.001.
Values may be sent and summed in bfloat16 or wider, within the bound.
No kernel may reach another device: no remote copies, remote signals or barrier semaphores. Data moves between devices by JAX's collectives and lax.ppermute only.
A program may use at most 32 MiB of HBM per device.

```python
import math
import jax
import jax.numpy as jnp

D = 5120
KVD = 1024
BLOCK = 128
TOK_DEV = 512
GROUPS = 128
TOKENS = 65536


def draw_lengths(key, part):
    key = jax.random.fold_in(key, 7)
    full = TOK_DEV // BLOCK
    first, second = jax.random.split(key)
    light = jax.random.randint(first, (GROUPS,), 1, full // 2 + 1)
    heavy = jax.random.randint(second, (GROUPS,), 0, 3) == 0
    blocks = jnp.where(heavy, full, light)
    blocks = blocks.at[0].set(full).at[1].set(1)
    return (blocks * BLOCK).astype(jnp.int32)


def raised(values, own_key, source, target, shards_of, factor):
    def block_of(dim):
        return (jnp.arange(values.shape[dim]) // (values.shape[dim] // shards_of)).reshape((-1,) + (1,) * (values.ndim - 1 - dim))

    one_side = jax.random.permutation(own_key, shards_of)[block_of(target)]
    other_side = (block_of(target) + shards_of // 2) % shards_of
    return jnp.where((block_of(source) == one_side) | (block_of(source) == other_side), factor * values, values)


def level_of(rng, shape, cuts, least, largest):
    gain, own = 1.0, jax.random.fold_in(rng, 6)
    for position, blocks in cuts:
        heights = jnp.exp(jax.random.uniform(jax.random.fold_in(own, position), (blocks,), jnp.float32, least / len(cuts), largest / len(cuts)))
        gain = gain * jnp.repeat(heights, shape[position] // blocks).reshape([-1 if axis == position else 1 for axis in range(len(shape))])
    return gain


def bell_draw(key, dims, spread, bound, cuts=(), kind=jnp.bfloat16):
    entries = jax.random.normal(key, dims, jnp.float32) * spread
    if len(cuts) > 0:
        entries = level_of(key, dims, cuts, -0.22, 0.18) * entries
    return jnp.clip(entries, min=-bound, max=bound).astype(kind)


def noise_with(key, dims, width, reach, cuts, heavy, kind=jnp.bfloat16):
    values = width * jax.random.normal(key, dims, jnp.float32)
    if cuts:
        values = values * level_of(key, dims, cuts, -0.22, 0.18)
    return jnp.clip(raised(values, jax.random.fold_in(key, 3), *heavy), -reach, reach).astype(kind)


def setup_inputs(seed: int = 0) -> dict:
    key_list = jax.random.split(jax.random.key(seed), 5)
    return {
        "saved_x": bell_draw(key_list[0], (TOKENS, D), 1.0, 6.0, ((0, 128), (1, 8))),
        "grad_key": noise_with(key_list[1], (TOKENS, KVD), 1.0, 24.0, ((0, 128), (1, 8)), (0, 1, 128, 5.5)),
        "w_key": bell_draw(key_list[2], (KVD, D), KVD ** -0.5, 0.1875, ((0, 128), (1, 8))),
        "lengths": draw_lengths(jax.random.fold_in(key_list[4], 71), 0),
    }


def reference(saved_x, grad_key, w_key, lengths):
    slots = jnp.arange(TOKENS, dtype=jnp.int32)
    owner = slots // TOK_DEV
    live = slots % TOK_DEV < lengths[owner]
    masked = jnp.where(live[:, None], grad_key, jnp.zeros_like(grad_key))
    grad_input = jnp.dot(masked, w_key, preferred_element_type=jnp.float32).astype(jnp.bfloat16)
    grad_weight = jnp.dot(masked.T, saved_x, preferred_element_type=jnp.float32) * (1.0 / math.sqrt(TOKENS))
    return (grad_input, grad_weight)
```

```python
import functools
import math

import jax
import jax.numpy as jnp
from jax import lax
from jax.experimental import pallas as pl
from jax.experimental.pallas import tpu as pltpu
from jax.sharding import Mesh, PartitionSpec as P

STEPS = 256.0
LARGEST = 32767.0
VMEM = pl.BlockSpec(memory_space=pltpu.VMEM)


def grads_kernel(g_ref, x_ref, own_ref, oth_ref):
    half = own_ref.shape[1]

    def block(k, _):
        d = lax.dot_general(g_ref[k], x_ref[...], (((0,), (0,)), ((), ())), preferred_element_type=jnp.float32)
        oth_ref[k] = d[half:]
        own_ref[k] = d[:half]
        return 0

    lax.fori_loop(0, g_ref.shape[0], block, 0)


def input_kernel(g_ref, own_ref, oth_ref, out_ref, w_ref):
    blocks, rows, width = g_ref.shape
    half = width // 2
    for k in range(blocks):
        w_ref[k * width : k * width + half, :] = own_ref[k * half : (k + 1) * half, :]
        w_ref[k * width + half : (k + 1) * width, :] = oth_ref[k * half : (k + 1) * half, :]
    part = min(rows, 128)

    def run(i, _):
        at = pl.ds(pl.multiple_of(i * part, part), part)
        g = jnp.concatenate([g_ref[k, at, :] for k in range(blocks)], axis=1)
        out_ref[at, :] = jnp.dot(g, w_ref[...], preferred_element_type=jnp.float32).astype(out_ref.dtype)
        return 0

    lax.fori_loop(0, rows // part, run, 0)


def pack_kernel(a_ref, b_ref, out_ref):
    width = a_ref.shape[2]
    lanes = out_ref.shape[2] - width

    def run(k, _):
        v = a_ref[k] + b_ref[k]
        top = jnp.maximum(jnp.max(jnp.abs(v), axis=1, keepdims=True), 1e-30)
        e = jnp.ceil(STEPS * jnp.log2(top * (1.0 / LARGEST))) + 1.0
        q = jnp.round(v * jnp.exp2(e * (-1.0 / STEPS)))
        out_ref[k, :, :width] = q.astype(jnp.int32).astype(jnp.int16)
        out_ref[k, :, width:] = jnp.broadcast_to(e, (v.shape[0], lanes)).astype(jnp.int32).astype(jnp.int16)
        return 0

    lax.fori_loop(0, a_ref.shape[0], run, 0)


def sum_kernel(scale, in_ref, out_ref):
    sources, rows, whole = in_ref.shape
    width = out_ref.shape[1]
    lanes = whole - width
    out_ref[...] = jnp.zeros_like(out_ref)
    part = min(8, sources)

    def run(k, _):
        total = [jnp.zeros((rows, lanes), jnp.float32) for _ in range(width // lanes)]
        for j in range(part):
            s = k * part + j
            step = jnp.exp2(in_ref[s, :, width:].astype(jnp.int32).astype(jnp.float32) * (1.0 / STEPS))
            for t in range(width // lanes):
                q = in_ref[s, :, t * lanes : (t + 1) * lanes].astype(jnp.int32).astype(jnp.float32)
                total[t] = total[t] + q * step
        for t in range(width // lanes):
            out_ref[:, t * lanes : (t + 1) * lanes] += total[t] * scale
        return 0

    lax.fori_loop(0, sources // part, run, 0)


def call(kernel, shapes, n, name, scratch=(), flops=0, moved=0):
    return pl.pallas_call(
        kernel,
        out_shape=shapes,
        in_specs=[VMEM] * n,
        out_specs=[VMEM] * len(shapes) if isinstance(shapes, (list, tuple)) else VMEM,
        scratch_shapes=scratch,
        compiler_params=pltpu.CompilerParams(vmem_limit_bytes=12 * 1024 * 1024),
        cost_estimate=pl.CostEstimate(flops=flops, bytes_accessed=moved, transcendentals=0),
        name=name,
    )


def merge_kernel(upper_ref, held_ref, got_ref, out_ref):
    upper = upper_ref[0]
    out_ref[:, pl.ds(upper, 1)] = held_ref[...][:, None]
    out_ref[:, pl.ds(1 - upper, 1)] = got_ref[...][:, None]


def double(held, axis, size, distances):
    for far in distances:
        got = lax.ppermute(held, axis, [(i, i ^ far) for i in range(size)])
        upper = (lax.axis_index(axis) // far) % 2
        count, rows, width = held.shape
        held = pl.pallas_call(
            merge_kernel,
            out_shape=jax.ShapeDtypeStruct((count, 2, rows, width), held.dtype),
            in_specs=[pl.BlockSpec(memory_space=pltpu.SMEM), VMEM, VMEM],
            out_specs=VMEM,
            compiler_params=pltpu.CompilerParams(vmem_limit_bytes=4 * 1024 * 1024),
            name="merge",
        )(upper.astype(jnp.int32).reshape(1), held, got).reshape(2 * count, rows, width)
    return held


def per_device(nz, nx, ny, x, g, w, lengths):
    rows, width = x.shape
    block = g.shape[1]
    half = block // 2
    core = lax.axis_index("c")
    group = (lax.axis_index("z") * nx + lax.axis_index("x")) * 2 + core

    x_steps = [nx >> i for i in range(1, nx.bit_length())]
    own = double(w[None], "z", nz, [nz >> i for i in range(1, nz.bit_length())])
    own = double(own, "x", nx, x_steps[:-2])

    live = jnp.arange(rows, dtype=jnp.int32) < lengths[group]
    masked = jnp.where(live[:, None], g, jnp.zeros_like(g))
    place = jnp.arange(block, dtype=jnp.int32)
    inner = place % half
    source = (inner // 8) * 16 + inner % 8 + 8 * jnp.where(place < half, core, 1 - core)
    order = (place[:, None] == source[None, :]).astype(g.dtype)
    sorted_g = jnp.dot(masked, order, preferred_element_type=jnp.float32).astype(g.dtype)
    grads = lax.all_to_all(jnp.broadcast_to(sorted_g[None], (ny,) + g.shape), "tensor", 0, 0)

    grads, own = lax.optimization_barrier((grads, own))
    own = double(own, "x", nx, x_steps[-2:-1])

    other_core = [(0, 1), (1, 0)]

    f32 = jax.ShapeDtypeStruct((ny, half, width), jnp.float32)
    mine, others = call(
        grads_kernel, (f32, f32), 2, "weight_grads", flops=2 * rows * ny * block * width, moved=6_000_000
    )(grads, x)
    got = lax.ppermute(others, "c", other_core)

    lanes = min(128, width)
    code = call(
        pack_kernel,
        jax.ShapeDtypeStruct((ny, half, width + lanes), jnp.int16),
        2,
        "pack",
        moved=4_000_000,
    )(mine, got)
    code, own = lax.optimization_barrier((code, own))
    code = lax.all_to_all(code.reshape(nz * nx, 8, width + lanes), ("z", "x"), 0, 0)
    scale = 1.0 / math.sqrt(rows * nz * nx * 2)
    grad_weight = call(
        functools.partial(sum_kernel, scale), jax.ShapeDtypeStruct((8, width), jnp.float32), 1, "unpack_sum", moved=1_000_000
    )(code)

    own = double(own, "x", nx, x_steps[-1:]).reshape(nz * half, width)
    oth = lax.ppermute(own, "c", other_core)
    grad_input = call(
        input_kernel,
        jax.ShapeDtypeStruct((rows, width), jnp.bfloat16),
        3,
        "input_grads",
        scratch=[pltpu.VMEM((ny * block, width), jnp.bfloat16)],
        flops=2 * rows * ny * block * width,
        moved=6_000_000,
    )(grads, own, oth)
    return (grad_input, grad_weight)


def solution(mesh):
    dp, ny = mesh.shape["dp"], mesh.shape["tensor"]
    nz, nx = ny, dp // (2 * ny)
    fine = Mesh(mesh.devices.reshape(nz, nx, 2, ny), ("z", "x", "c", "tensor"))
    both = P(("z", "x", "c"), "tensor")
    return jax.shard_map(
        functools.partial(per_device, nz, nx, ny),
        mesh=fine,
        in_specs=(both, both, both, P()),
        out_specs=(both, both),
        check_vma=False,
    )
```

```python
import functools
import math

import jax
import jax.numpy as jnp
from jax import lax
from jax.experimental import pallas as pl
from jax.experimental.pallas import tpu as pltpu
from jax.sharding import Mesh, PartitionSpec as P

STEPS = 256.0
LARGEST = 32767.0
BIAS = 127.0
VMEM = pl.BlockSpec(memory_space=pltpu.VMEM)
SMEM = pl.BlockSpec(memory_space=pltpu.SMEM)


def sort_kernel(lengths_ref, place_ref, g_ref, out_ref):
    rows, width = g_ref.shape
    half = width // 2
    core = place_ref[0] % 2
    length = lengths_ref[place_ref[0]]
    take = lax.broadcasted_iota(jnp.int32, (width, width), 0)
    place = lax.broadcasted_iota(jnp.int32, (width, width), 1)
    inner = place % half
    kind = jnp.where(place < half, core, 1 - core)
    order = jnp.where(take == (inner // 8) * 16 + inner % 8 + 8 * kind, 1.0, 0.0).astype(g_ref.dtype)
    g = jnp.dot(g_ref[...], order, preferred_element_type=jnp.float32)
    live = lax.broadcasted_iota(jnp.int32, (rows, width), 0) < length
    g = jnp.where(live, g, 0.0).astype(out_ref.dtype)
    for k in range(out_ref.shape[0]):
        out_ref[k] = g


def other_kernel(g_ref, x_ref, oth_ref, own_ref, turned_ref):
    blocks, rows, width = g_ref.shape
    half = width // 2
    for k in range(blocks):
        turned = g_ref[k].T
        own_ref[k * half : (k + 1) * half, :] = turned[:half]
        turned_ref[k * half : (k + 1) * half, :] = turned[half:]
    oth_ref[...] = jnp.dot(turned_ref[...], x_ref[...], preferred_element_type=jnp.float32)


def own_kernel(g_ref, x_ref, out_ref):
    out_ref[...] = jnp.dot(g_ref[...], x_ref[...], preferred_element_type=jnp.float32)


def pack_kernel(a_ref, b_ref, w_ref, out_ref):
    rows, width = w_ref.shape
    lanes = out_ref.shape[2] - 2 * width

    def store(k, at, v):
        out_ref[k, :, at : at + v.shape[1]] = v.astype(jnp.int32).astype(out_ref.dtype)

    w = w_ref[...].astype(jnp.float32)
    size = jnp.abs(w)
    e = jnp.floor(jnp.log2(jnp.maximum(size, 2.0**-126)))
    bits = (e + BIAS) * 128.0 + (size * jnp.exp2(-e) * 128.0 - 128.0)
    bits = jnp.where(size < 2.0**-126, 0.0, bits)
    bits = jnp.round(jnp.where(w < 0.0, -bits, bits))
    for k in range(out_ref.shape[0]):
        v = a_ref[k] + b_ref[k]
        top = jnp.maximum(jnp.max(jnp.abs(v), axis=1, keepdims=True), 1e-30)
        e = jnp.ceil(STEPS * jnp.log2(top * (1.0 / LARGEST))) + 1.0
        store(k, 0, jnp.round(v * jnp.exp2(e * (-1.0 / STEPS))))
        store(k, width, jnp.broadcast_to(e, (rows, lanes)))
        store(k, width + lanes, bits)


def weights_kernel(in_ref, out_ref):
    width = out_ref.shape[2]
    for s in range(in_ref.shape[0]):
        bits = in_ref[s, :, in_ref.shape[2] - width :].astype(jnp.int32)
        size = jnp.abs(bits)
        e = (size >> 7).astype(jnp.float32) - BIAS
        v = ((size & 127) + 128).astype(jnp.float32) * jnp.exp2(e) * (1.0 / 128.0)
        v = jnp.where(size < 128, 0.0, jnp.where(bits < 0, -v, v))
        out_ref[s] = v.astype(out_ref.dtype)


def sum_kernel(scale, in_ref, out_ref):
    rows, width = out_ref.shape
    lanes = in_ref.shape[2] - 2 * width
    total = [jnp.zeros((rows, lanes), jnp.float32) for _ in range(width // lanes)]
    for s in range(in_ref.shape[0]):
        step = jnp.exp2(in_ref[s, :, width : width + lanes].astype(jnp.int32).astype(jnp.float32) * (1.0 / STEPS))
        for t in range(width // lanes):
            q = in_ref[s, :, t * lanes : (t + 1) * lanes].astype(jnp.int32).astype(jnp.float32)
            total[t] = total[t] + q * step
    for t in range(width // lanes):
        out_ref[:, t * lanes : (t + 1) * lanes] = total[t] * scale


def input_kernel(g_ref, own_ref, oth_ref, out_ref, w_ref):
    blocks, rows, width = g_ref.shape
    half = width // 2
    for k in range(blocks):
        w_ref[k * width : k * width + half, :] = own_ref[k * half : (k + 1) * half, :]
        w_ref[k * width + half : (k + 1) * width, :] = oth_ref[k * half : (k + 1) * half, :]
    g = jnp.concatenate([g_ref[k] for k in range(blocks)], axis=1)
    out_ref[...] = jnp.dot(g, w_ref[...], preferred_element_type=jnp.float32).astype(out_ref.dtype)


def call(kernel, out, specs, name, scratch=(), flops=0, moved=0):
    return pl.pallas_call(
        kernel,
        out_shape=[jax.ShapeDtypeStruct(*o) for o in out],
        in_specs=specs,
        out_specs=[VMEM] * len(out),
        scratch_shapes=scratch,
        compiler_params=pltpu.CompilerParams(vmem_limit_bytes=14 * 1024 * 1024),
        cost_estimate=pl.CostEstimate(flops=flops, bytes_accessed=moved, transcendentals=0),
        name=name,
    )


def per_device(nz, nx, ny, x, g, w, lengths):
    rows, width = x.shape
    block = g.shape[1]
    half = block // 2
    features = ny * half
    lanes = 128
    work = 2 * rows * features * width
    group = (lax.axis_index("z") * nx + lax.axis_index("x")) * 2 + lax.axis_index("c")
    swap = [(0, 1), (1, 0)]

    (copies,) = call(sort_kernel, [((ny, rows, block), g.dtype)], [SMEM, SMEM, VMEM], "sort", moved=2_000_000)(
        lengths, group.astype(jnp.int32).reshape(1), g
    )
    grads = lax.all_to_all(copies, "tensor", 0, 0)

    oth, turned = call(
        other_kernel,
        [((features, width), jnp.float32), ((features, rows), g.dtype)],
        [VMEM, VMEM],
        "weight_grads_other",
        scratch=[pltpu.VMEM((features, rows), g.dtype)],
        flops=work,
        moved=3_000_000,
    )(grads, x)
    got = lax.ppermute(oth, "c", swap)
    (mine,) = call(
        own_kernel, [((features, width), jnp.float32)], [VMEM, VMEM], "weight_grads_own", flops=work, moved=3_000_000
    )(turned, x)

    peers = nz * nx
    (code,) = call(pack_kernel, [((peers, 8, 2 * width + lanes), jnp.int16)], [VMEM] * 3, "pack", moved=4_000_000)(
        mine.reshape(peers, 8, width), got.reshape(peers, 8, width), w
    )
    code = lax.all_to_all(code, ("z", "x"), 0, 0)
    (own_w,) = call(weights_kernel, [((peers, 8, width), w.dtype)], [VMEM], "unpack_weights", moved=1_500_000)(code)
    own_w = own_w.reshape(features, width)
    oth_w = lax.ppermute(own_w, "c", swap)
    scale = 1.0 / math.sqrt(rows * peers * 2)
    (grad_weight,) = call(
        functools.partial(sum_kernel, scale), [((8, width), jnp.float32)], [VMEM], "unpack_sum", moved=1_000_000
    )(code)
    (grad_input,) = call(
        input_kernel,
        [((rows, width), jnp.bfloat16)],
        [VMEM] * 3,
        "input_grads",
        scratch=[pltpu.VMEM((2 * features, width), w.dtype)],
        flops=2 * work,
        moved=4_000_000,
    )(grads, own_w, oth_w)
    return (grad_input, grad_weight)


def solution(mesh):
    dp, ny = mesh.shape["dp"], mesh.shape["tensor"]
    nz, nx = ny, dp // (2 * ny)
    fine = Mesh(mesh.devices.reshape(nz, nx, 2, ny), ("z", "x", "c", "tensor"))
    both = P(("z", "x", "c"), "tensor")
    return jax.shard_map(
        functools.partial(per_device, nz, nx, ny),
        mesh=fine,
        in_specs=(both, both, both, P()),
        out_specs=(both, both),
        check_vma=False,
    )
```

```python
import functools
import math

import jax
import jax.numpy as jnp
from jax import lax
from jax.experimental import pallas as pl
from jax.experimental.pallas import tpu as pltpu
from jax.sharding import Mesh, PartitionSpec as P

STEPS = 256.0
LARGEST = 32767.0
VMEM = pl.BlockSpec(memory_space=pltpu.VMEM)
SMEM = pl.BlockSpec(memory_space=pltpu.SMEM)


def sort_kernel(lengths_ref, place_ref, g_ref, out_ref):
    rows, width = g_ref.shape
    half = width // 2
    core = place_ref[0] % 2
    length = lengths_ref[place_ref[0]]
    take = lax.broadcasted_iota(jnp.int32, (width, width), 0)
    place = lax.broadcasted_iota(jnp.int32, (width, width), 1)
    inner = place % half
    kind = jnp.where(place < half, core, 1 - core)
    order = jnp.where(take == (inner // 8) * 16 + inner % 8 + 8 * kind, 1.0, 0.0).astype(g_ref.dtype)
    g = jnp.dot(g_ref[...], order, preferred_element_type=jnp.float32)
    live = lax.broadcasted_iota(jnp.int32, (rows, width), 0) < length
    g = jnp.where(live, g, 0.0).astype(out_ref.dtype)
    for k in range(out_ref.shape[0]):
        out_ref[k] = g


def other_kernel(g_ref, x_ref, oth_ref, own_ref, turned_ref):
    blocks, rows, width = g_ref.shape
    half = width // 2
    for k in range(blocks):
        turned = g_ref[k].T
        own_ref[k * half : (k + 1) * half, :] = turned[:half]
        turned_ref[k * half : (k + 1) * half, :] = turned[half:]
    oth_ref[...] = jnp.dot(turned_ref[...], x_ref[...], preferred_element_type=jnp.float32)


def own_kernel(g_ref, x_ref, out_ref):
    out_ref[...] = jnp.dot(g_ref[...], x_ref[...], preferred_element_type=jnp.float32)


def pack_kernel(a_ref, b_ref, out_ref):
    _, rows, width = a_ref.shape
    lanes = out_ref.shape[2] - width
    for k in range(out_ref.shape[0]):
        v = a_ref[k] + b_ref[k]
        top = jnp.maximum(jnp.max(jnp.abs(v), axis=1, keepdims=True), 1e-30)
        e = jnp.ceil(STEPS * jnp.log2(top * (1.0 / LARGEST))) + 1.0
        q = jnp.round(v * jnp.exp2(e * (-1.0 / STEPS)))
        out_ref[k, :, :width] = q.astype(jnp.int32).astype(out_ref.dtype)
        out_ref[k, :, width:] = jnp.broadcast_to(e, (rows, lanes)).astype(jnp.int32).astype(out_ref.dtype)


def sum_kernel(scale, in_ref, out_ref):
    rows, width = out_ref.shape
    lanes = in_ref.shape[2] - width
    total = [jnp.zeros((rows, lanes), jnp.float32) for _ in range(width // lanes)]
    for s in range(in_ref.shape[0]):
        step = jnp.exp2(in_ref[s, :, width : width + lanes].astype(jnp.int32).astype(jnp.float32) * (1.0 / STEPS))
        for t in range(width // lanes):
            q = in_ref[s, :, t * lanes : (t + 1) * lanes].astype(jnp.int32).astype(jnp.float32)
            total[t] = total[t] + q * step
    for t in range(width // lanes):
        out_ref[:, t * lanes : (t + 1) * lanes] = total[t] * scale


def input_kernel(g_ref, own_ref, oth_ref, out_ref, w_ref):
    blocks, rows, width = g_ref.shape
    half = width // 2
    for k in range(blocks):
        w_ref[k * width : k * width + half, :] = own_ref[k * half : (k + 1) * half, :]
        w_ref[k * width + half : (k + 1) * width, :] = oth_ref[k * half : (k + 1) * half, :]
    g = jnp.concatenate([g_ref[k] for k in range(blocks)], axis=1)
    out_ref[...] = jnp.dot(g, w_ref[...], preferred_element_type=jnp.float32).astype(out_ref.dtype)


def call(kernel, out, specs, name, scratch=(), flops=0, moved=0):
    return pl.pallas_call(
        kernel,
        out_shape=[jax.ShapeDtypeStruct(*o) for o in out],
        in_specs=specs,
        out_specs=[VMEM] * len(out),
        scratch_shapes=scratch,
        compiler_params=pltpu.CompilerParams(vmem_limit_bytes=14 * 1024 * 1024),
        cost_estimate=pl.CostEstimate(flops=flops, bytes_accessed=moved, transcendentals=0),
        name=name,
    )


def per_device(nz, nx, ny, x, g, w, lengths):
    rows, width = x.shape
    block = g.shape[1]
    half = block // 2
    features = ny * half
    lanes = 128
    work = 2 * rows * features * width
    group = (lax.axis_index("z") * nx + lax.axis_index("x")) * 2 + lax.axis_index("c")
    swap = [(0, 1), (1, 0)]

    (copies,) = call(sort_kernel, [((ny, rows, block), g.dtype)], [SMEM, SMEM, VMEM], "sort", moved=2_000_000)(
        lengths, group.astype(jnp.int32).reshape(1), g
    )
    grads = lax.all_to_all(copies, "tensor", 0, 0)
    line = lax.all_gather(w, "x", axis=0, tiled=True)
    grads, line = lax.optimization_barrier((grads, line))

    oth, turned = call(
        other_kernel,
        [((features, width), jnp.float32), ((features, rows), g.dtype)],
        [VMEM, VMEM],
        "weight_grads_other",
        scratch=[pltpu.VMEM((features, rows), g.dtype)],
        flops=work,
        moved=3_000_000,
    )(grads, x)
    got = lax.ppermute(oth, "c", swap)
    (mine,) = call(
        own_kernel, [((features, width), jnp.float32)], [VMEM, VMEM], "weight_grads_own", flops=work, moved=3_000_000
    )(turned, x)

    peers = nz * nx
    (code,) = call(pack_kernel, [((peers, 8, width + lanes), jnp.int16)], [VMEM] * 2, "pack", moved=4_000_000)(
        mine.reshape(peers, 8, width), got.reshape(peers, 8, width)
    )
    code = lax.all_to_all(code, ("z", "x"), 0, 0)
    own_w = lax.all_gather(line, "z", axis=0, tiled=True)
    oth_w = lax.ppermute(own_w, "c", swap)
    scale = 1.0 / math.sqrt(rows * peers * 2)
    (grad_weight,) = call(
        functools.partial(sum_kernel, scale), [((8, width), jnp.float32)], [VMEM], "unpack_sum", moved=1_000_000
    )(code)
    (grad_input,) = call(
        input_kernel,
        [((rows, width), jnp.bfloat16)],
        [VMEM] * 3,
        "input_grads",
        scratch=[pltpu.VMEM((2 * features, width), w.dtype)],
        flops=2 * work,
        moved=4_000_000,
    )(grads, own_w, oth_w)
    return (grad_input, grad_weight)


def solution(mesh):
    dp, ny = mesh.shape["dp"], mesh.shape["tensor"]
    nz, nx = ny, dp // (2 * ny)
    fine = Mesh(mesh.devices.reshape(nz, nx, 2, ny), ("z", "x", "c", "tensor"))
    both = P(("z", "x", "c"), "tensor")
    return jax.shard_map(
        functools.partial(per_device, nz, nx, ny),
        mesh=fine,
        in_specs=(both, both, both, P()),
        out_specs=(both, both),
        check_vma=False,
    )
```

```python
import functools
import math

import jax
import jax.numpy as jnp
from jax import lax
from jax.experimental import pallas as pl
from jax.experimental.pallas import tpu as pltpu
from jax.sharding import Mesh, PartitionSpec as P

STEPS = 256.0
LARGEST = 32767.0
VMEM = pl.BlockSpec(memory_space=pltpu.VMEM)
SMEM = pl.BlockSpec(memory_space=pltpu.SMEM)


def sort_kernel(lengths_ref, place_ref, g_ref, out_ref):
    rows, width = g_ref.shape
    half = width // 2
    core = place_ref[0] % 2
    length = lengths_ref[place_ref[0]]
    take = lax.broadcasted_iota(jnp.int32, (width, width), 0)
    place = lax.broadcasted_iota(jnp.int32, (width, width), 1)
    inner = place % half
    kind = jnp.where(place < half, core, 1 - core)
    order = jnp.where(take == (inner // 8) * 16 + inner % 8 + 8 * kind, 1.0, 0.0).astype(g_ref.dtype)
    g = jnp.dot(g_ref[...], order, preferred_element_type=jnp.float32)
    live = lax.broadcasted_iota(jnp.int32, (rows, width), 0) < length
    g = jnp.where(live, g, 0.0).astype(out_ref.dtype)
    for k in range(out_ref.shape[0]):
        out_ref[k] = g


def other_kernel(g_ref, x_ref, oth_ref, own_ref, turned_ref):
    blocks, rows, width = g_ref.shape
    half = width // 2
    for k in range(blocks):
        turned = g_ref[k].T
        own_ref[k * half : (k + 1) * half, :] = turned[:half]
        turned_ref[k * half : (k + 1) * half, :] = turned[half:]
    oth_ref[...] = jnp.dot(turned_ref[...], x_ref[...], preferred_element_type=jnp.float32)


def own_kernel(g_ref, x_ref, out_ref):
    out_ref[...] = jnp.dot(g_ref[...], x_ref[...], preferred_element_type=jnp.float32)


def pack_kernel(a_ref, b_ref, out_ref):
    _, rows, width = a_ref.shape
    lanes = out_ref.shape[2] - width
    for k in range(out_ref.shape[0]):
        v = a_ref[k] + b_ref[k]
        top = jnp.maximum(jnp.max(jnp.abs(v), axis=1, keepdims=True), 1e-30)
        e = jnp.ceil(STEPS * jnp.log2(top * (1.0 / LARGEST))) + 1.0
        q = jnp.round(v * jnp.exp2(e * (-1.0 / STEPS)))
        out_ref[k, :, :width] = q.astype(jnp.int32).astype(out_ref.dtype)
        out_ref[k, :, width:] = jnp.broadcast_to(e, (rows, lanes)).astype(jnp.int32).astype(out_ref.dtype)


def sum_kernel(scale, in_ref, out_ref):
    rows, width = out_ref.shape
    lanes = in_ref.shape[2] - width
    total = [jnp.zeros((rows, lanes), jnp.float32) for _ in range(width // lanes)]
    for s in range(in_ref.shape[0]):
        step = jnp.exp2(in_ref[s, :, width : width + lanes].astype(jnp.int32).astype(jnp.float32) * (1.0 / STEPS))
        for t in range(width // lanes):
            q = in_ref[s, :, t * lanes : (t + 1) * lanes].astype(jnp.int32).astype(jnp.float32)
            total[t] = total[t] + q * step
    for t in range(width // lanes):
        out_ref[:, t * lanes : (t + 1) * lanes] = total[t] * scale


def input_kernel(g_ref, own_ref, oth_ref, out_ref, w_ref):
    blocks, rows, width = g_ref.shape
    half = width // 2
    for k in range(blocks):
        w_ref[k * width : k * width + half, :] = own_ref[k * half : (k + 1) * half, :]
        w_ref[k * width + half : (k + 1) * width, :] = oth_ref[k * half : (k + 1) * half, :]
    g = jnp.concatenate([g_ref[k] for k in range(blocks)], axis=1)
    out_ref[...] = jnp.dot(g, w_ref[...], preferred_element_type=jnp.float32).astype(out_ref.dtype)


def call(kernel, out, specs, name, scratch=(), flops=0, moved=0):
    return pl.pallas_call(
        kernel,
        out_shape=[jax.ShapeDtypeStruct(*o) for o in out],
        in_specs=specs,
        out_specs=[VMEM] * len(out),
        scratch_shapes=scratch,
        compiler_params=pltpu.CompilerParams(vmem_limit_bytes=14 * 1024 * 1024),
        cost_estimate=pl.CostEstimate(flops=flops, bytes_accessed=moved, transcendentals=0),
        name=name,
    )


def per_device(nz, nx, ny, x, g, w, lengths):
    rows, width = x.shape
    block = g.shape[1]
    half = block // 2
    features = ny * half
    lanes = 128
    work = 2 * rows * features * width
    group = (lax.axis_index("z") * nx + lax.axis_index("x")) * 2 + lax.axis_index("c")
    swap = [(0, 1), (1, 0)]

    (copies,) = call(sort_kernel, [((ny, rows, block), g.dtype)], [SMEM, SMEM, VMEM], "sort", moved=2_000_000)(
        lengths, group.astype(jnp.int32).reshape(1), g
    )
    grads = lax.all_to_all(copies, "tensor", 0, 0)
    own_w = lax.all_gather(w, ("z", "x"), axis=0, tiled=True)
    grads, own_w = lax.optimization_barrier((grads, own_w))

    oth, turned = call(
        other_kernel,
        [((features, width), jnp.float32), ((features, rows), g.dtype)],
        [VMEM, VMEM],
        "weight_grads_other",
        scratch=[pltpu.VMEM((features, rows), g.dtype)],
        flops=work,
        moved=3_000_000,
    )(grads, x)
    got = lax.ppermute(oth, "c", swap)
    (mine,) = call(
        own_kernel, [((features, width), jnp.float32)], [VMEM, VMEM], "weight_grads_own", flops=work, moved=3_000_000
    )(turned, x)

    peers = nz * nx
    (code,) = call(pack_kernel, [((peers, 8, width + lanes), jnp.int16)], [VMEM] * 2, "pack", moved=4_000_000)(
        mine.reshape(peers, 8, width), got.reshape(peers, 8, width)
    )
    code, own_w = lax.optimization_barrier((code, own_w))
    code = lax.all_to_all(code, ("z", "x"), 0, 0)
    oth_w = lax.ppermute(own_w, "c", swap)
    scale = 1.0 / math.sqrt(rows * peers * 2)
    (grad_weight,) = call(
        functools.partial(sum_kernel, scale), [((8, width), jnp.float32)], [VMEM], "unpack_sum", moved=1_000_000
    )(code)
    (grad_input,) = call(
        input_kernel,
        [((rows, width), jnp.bfloat16)],
        [VMEM] * 3,
        "input_grads",
        scratch=[pltpu.VMEM((2 * features, width), w.dtype)],
        flops=2 * work,
        moved=4_000_000,
    )(grads, own_w, oth_w)
    return (grad_input, grad_weight)


def solution(mesh):
    dp, ny = mesh.shape["dp"], mesh.shape["tensor"]
    nz, nx = ny, dp // (2 * ny)
    fine = Mesh(mesh.devices.reshape(nz, nx, 2, ny), ("z", "x", "c", "tensor"))
    both = P(("z", "x", "c"), "tensor")
    return jax.shard_map(
        functools.partial(per_device, nz, nx, ny),
        mesh=fine,
        in_specs=(both, both, both, P()),
        out_specs=(both, both),
        check_vma=False,
    )
```

```python
import functools
import math

import jax
import jax.numpy as jnp
from jax import lax
from jax.experimental import pallas as pl
from jax.experimental.pallas import tpu as pltpu
from jax.sharding import Mesh, PartitionSpec as P

STEPS = 256.0
LARGEST = 32767.0
VMEM = pl.BlockSpec(memory_space=pltpu.VMEM)
SMEM = pl.BlockSpec(memory_space=pltpu.SMEM)


def other_kernel(lengths_ref, place_ref, g_ref, x_ref, oth_ref, own_ref, sorted_ref, turned_ref):
    blocks, rows, width = g_ref.shape
    half = width // 2
    core = place_ref[0] % 2
    length = lengths_ref[place_ref[0]]
    take = lax.broadcasted_iota(jnp.int32, (width, width), 0)
    place = lax.broadcasted_iota(jnp.int32, (width, width), 1)
    inner = place % half
    kind = jnp.where(place < half, core, 1 - core)
    order = jnp.where(take == (inner // 8) * 16 + inner % 8 + 8 * kind, 1.0, 0.0).astype(g_ref.dtype)
    live = lax.broadcasted_iota(jnp.int32, (rows, width), 0) < length
    for k in range(blocks):
        g = jnp.dot(g_ref[k], order, preferred_element_type=jnp.float32)
        g = jnp.where(live, g, 0.0).astype(g_ref.dtype)
        sorted_ref[k] = g
        turned = g.T
        own_ref[k * half : (k + 1) * half, :] = turned[:half]
        turned_ref[k * half : (k + 1) * half, :] = turned[half:]
    oth_ref[...] = jnp.dot(turned_ref[...], x_ref[...], preferred_element_type=jnp.float32)


def own_kernel(g_ref, x_ref, out_ref):
    out_ref[...] = jnp.dot(g_ref[...], x_ref[...], preferred_element_type=jnp.float32)


def pack_kernel(a_ref, b_ref, out_ref):
    _, rows, width = a_ref.shape
    lanes = out_ref.shape[2] - width
    for k in range(out_ref.shape[0]):
        v = a_ref[k] + b_ref[k]
        top = jnp.maximum(jnp.max(jnp.abs(v), axis=1, keepdims=True), 1e-30)
        e = jnp.ceil(STEPS * jnp.log2(top * (1.0 / LARGEST))) + 1.0
        q = jnp.round(v * jnp.exp2(e * (-1.0 / STEPS)))
        out_ref[k, :, :width] = q.astype(jnp.int32).astype(out_ref.dtype)
        out_ref[k, :, width:] = jnp.broadcast_to(e, (rows, lanes)).astype(jnp.int32).astype(out_ref.dtype)


def sum_kernel(scale, in_ref, out_ref):
    rows, width = out_ref.shape
    lanes = in_ref.shape[2] - width
    total = [jnp.zeros((rows, lanes), jnp.float32) for _ in range(width // lanes)]
    for s in range(in_ref.shape[0]):
        step = jnp.exp2(in_ref[s, :, width : width + lanes].astype(jnp.int32).astype(jnp.float32) * (1.0 / STEPS))
        for t in range(width // lanes):
            q = in_ref[s, :, t * lanes : (t + 1) * lanes].astype(jnp.int32).astype(jnp.float32)
            total[t] = total[t] + q * step
    for t in range(width // lanes):
        out_ref[:, t * lanes : (t + 1) * lanes] = total[t] * scale


def input_kernel(g_ref, own_ref, oth_ref, out_ref, w_ref):
    blocks, rows, width = g_ref.shape
    half = width // 2
    for k in range(blocks):
        w_ref[k * width : k * width + half, :] = own_ref[k * half : (k + 1) * half, :]
        w_ref[k * width + half : (k + 1) * width, :] = oth_ref[k * half : (k + 1) * half, :]
    g = jnp.concatenate([g_ref[k] for k in range(blocks)], axis=1)
    out_ref[...] = jnp.dot(g, w_ref[...], preferred_element_type=jnp.float32).astype(out_ref.dtype)


def call(kernel, out, specs, name, scratch=(), flops=0, moved=0):
    return pl.pallas_call(
        kernel,
        out_shape=[jax.ShapeDtypeStruct(*o) for o in out],
        in_specs=specs,
        out_specs=[VMEM] * len(out),
        scratch_shapes=scratch,
        compiler_params=pltpu.CompilerParams(vmem_limit_bytes=14 * 1024 * 1024),
        cost_estimate=pl.CostEstimate(flops=flops, bytes_accessed=moved, transcendentals=0),
        name=name,
    )


def per_device(nz, nx, ny, x, g, w, lengths):
    rows, width = x.shape
    block = g.shape[1]
    half = block // 2
    features = ny * half
    lanes = 128
    work = 2 * rows * features * width
    group = (lax.axis_index("z") * nx + lax.axis_index("x")) * 2 + lax.axis_index("c")
    swap = [(0, 1), (1, 0)]

    grads = lax.all_gather(g, "tensor", axis=0, tiled=True)
    own_w = lax.all_to_all(jnp.broadcast_to(w[None], (nz * nx,) + w.shape), ("z", "x"), 0, 0).reshape(features, width)
    grads, own_w = lax.optimization_barrier((grads, own_w))

    oth, turned, grads = call(
        other_kernel,
        [((features, width), jnp.float32), ((features, rows), g.dtype), ((ny, rows, block), g.dtype)],
        [SMEM, SMEM, VMEM, VMEM],
        "weight_grads_other",
        scratch=[pltpu.VMEM((features, rows), g.dtype)],
        flops=work,
        moved=3_000_000,
    )(lengths, group.astype(jnp.int32).reshape(1), grads.reshape(ny, rows, block), x)
    got = lax.ppermute(oth, "c", swap)
    (mine,) = call(
        own_kernel, [((features, width), jnp.float32)], [VMEM, VMEM], "weight_grads_own", flops=work, moved=3_000_000
    )(turned, x)

    peers = nz * nx
    (code,) = call(pack_kernel, [((peers, 8, width + lanes), jnp.int16)], [VMEM] * 2, "pack", moved=4_000_000)(
        mine.reshape(peers, 8, width), got.reshape(peers, 8, width)
    )
    code, own_w = lax.optimization_barrier((code, own_w))
    code = lax.all_to_all(code, ("z", "x"), 0, 0)
    oth_w = lax.ppermute(own_w, "c", swap)
    scale = 1.0 / math.sqrt(rows * peers * 2)
    (grad_weight,) = call(
        functools.partial(sum_kernel, scale), [((8, width), jnp.float32)], [VMEM], "unpack_sum", moved=1_000_000
    )(code)
    (grad_input,) = call(
        input_kernel,
        [((rows, width), jnp.bfloat16)],
        [VMEM] * 3,
        "input_grads",
        scratch=[pltpu.VMEM((2 * features, width), w.dtype)],
        flops=2 * work,
        moved=4_000_000,
    )(grads, own_w, oth_w)
    return (grad_input, grad_weight)


def solution(mesh):
    dp, ny = mesh.shape["dp"], mesh.shape["tensor"]
    nz, nx = ny, dp // (2 * ny)
    fine = Mesh(mesh.devices.reshape(nz, nx, 2, ny), ("z", "x", "c", "tensor"))
    both = P(("z", "x", "c"), "tensor")
    return jax.shard_map(
        functools.partial(per_device, nz, nx, ny),
        mesh=fine,
        in_specs=(both, both, both, P()),
        out_specs=(both, both),
        check_vma=False,
    )
```

```python
import functools
import math

import jax
import jax.numpy as jnp
from jax import lax
from jax.experimental import pallas as pl
from jax.experimental.pallas import tpu as pltpu
from jax.sharding import Mesh, PartitionSpec as P

STEPS = 256.0
LARGEST = 32767.0
VMEM = pl.BlockSpec(memory_space=pltpu.VMEM)
SMEM = pl.BlockSpec(memory_space=pltpu.SMEM)


def other_kernel(lengths_ref, place_ref, g_ref, rest_ref, x_ref, oth_ref, own_ref, sorted_ref, turned_ref):
    blocks, _, width = g_ref.shape
    rows = x_ref.shape[0]
    bits = blocks.bit_length() - 1
    half = width // 2
    core = place_ref[0] % 2
    me = place_ref[1]
    length = lengths_ref[place_ref[0]]
    take = lax.broadcasted_iota(jnp.int32, (width, width), 0)
    place = lax.broadcasted_iota(jnp.int32, (width, width), 1)
    inner = place % half
    kind = jnp.where(place < half, core, 1 - core)
    order = jnp.where(take == (inner // 8) * 16 + inner % 8 + 8 * kind, 1.0, 0.0).astype(g_ref.dtype)
    live = lax.broadcasted_iota(jnp.int32, (rows, width), 0) < length
    for k in range(blocks):
        at = 0
        for b in range(bits):
            at = at + (((k >> b) % 2 + me // 2**b) % 2) * 2 ** (bits - 1 - b)
        parts = [g_ref[k], rest_ref[at]]
        g = jnp.concatenate([jnp.dot(p, order, preferred_element_type=jnp.float32) for p in parts], axis=0)
        g = jnp.where(live, g, 0.0).astype(g_ref.dtype)
        sorted_ref[k] = g
        turned = g.T
        own_ref[k * half : (k + 1) * half, :] = turned[:half]
        turned_ref[k * half : (k + 1) * half, :] = turned[half:]
    oth_ref[...] = jnp.dot(turned_ref[...], x_ref[...], preferred_element_type=jnp.float32)


def own_kernel(g_ref, x_ref, out_ref):
    out_ref[...] = jnp.dot(g_ref[...], x_ref[...], preferred_element_type=jnp.float32)


def pack_kernel(a_ref, b_ref, out_ref):
    _, rows, width = a_ref.shape
    lanes = out_ref.shape[2] - width
    for k in range(out_ref.shape[0]):
        v = a_ref[k] + b_ref[k]
        top = jnp.maximum(jnp.max(jnp.abs(v), axis=1, keepdims=True), 1e-30)
        e = jnp.ceil(STEPS * jnp.log2(top * (1.0 / LARGEST))) + 1.0
        q = jnp.round(v * jnp.exp2(e * (-1.0 / STEPS)))
        out_ref[k, :, :width] = q.astype(jnp.int32).astype(out_ref.dtype)
        out_ref[k, :, width:] = jnp.broadcast_to(e, (rows, lanes)).astype(jnp.int32).astype(out_ref.dtype)


def sum_kernel(scale, in_ref, out_ref):
    rows, width = out_ref.shape
    lanes = in_ref.shape[2] - width
    total = [jnp.zeros((rows, lanes), jnp.float32) for _ in range(width // lanes)]
    for s in range(in_ref.shape[0]):
        step = jnp.exp2(in_ref[s, :, width : width + lanes].astype(jnp.int32).astype(jnp.float32) * (1.0 / STEPS))
        for t in range(width // lanes):
            q = in_ref[s, :, t * lanes : (t + 1) * lanes].astype(jnp.int32).astype(jnp.float32)
            total[t] = total[t] + q * step
    for t in range(width // lanes):
        out_ref[:, t * lanes : (t + 1) * lanes] = total[t] * scale


def input_kernel(g_ref, own_ref, oth_ref, out_ref, w_ref):
    blocks, rows, width = g_ref.shape
    half = width // 2
    for k in range(blocks):
        w_ref[k * width : k * width + half, :] = own_ref[k * half : (k + 1) * half, :]
        w_ref[k * width + half : (k + 1) * width, :] = oth_ref[k * half : (k + 1) * half, :]
    g = jnp.concatenate([g_ref[k] for k in range(blocks)], axis=1)
    out_ref[...] = jnp.dot(g, w_ref[...], preferred_element_type=jnp.float32).astype(out_ref.dtype)


def call(kernel, out, specs, name, scratch=(), flops=0, moved=0):
    return pl.pallas_call(
        kernel,
        out_shape=[jax.ShapeDtypeStruct(*o) for o in out],
        in_specs=specs,
        out_specs=[VMEM] * len(out),
        scratch_shapes=scratch,
        compiler_params=pltpu.CompilerParams(vmem_limit_bytes=14 * 1024 * 1024),
        cost_estimate=pl.CostEstimate(flops=flops, bytes_accessed=moved, transcendentals=0),
        name=name,
    )


def per_device(nz, nx, ny, x, g, w, lengths):
    rows, width = x.shape
    block = g.shape[1]
    half = block // 2
    features = ny * half
    lanes = 128
    work = 2 * rows * features * width
    group = (lax.axis_index("z") * nx + lax.axis_index("x")) * 2 + lax.axis_index("c")
    swap = [(0, 1), (1, 0)]

    rest = min(16, rows // 2)
    ends = g[None, rows - rest :]
    far = ny // 2
    while far:
        ends = jnp.concatenate([ends, lax.ppermute(ends, "tensor", [(i, i ^ far) for i in range(ny)])], axis=0)
        far //= 2
    grads = lax.all_gather(g[: rows - rest], "tensor", axis=0, tiled=False)
    own_w = lax.all_to_all(jnp.broadcast_to(w[None], (nz * nx,) + w.shape), ("z", "x"), 0, 0).reshape(features, width)
    grads, ends, own_w = lax.optimization_barrier((grads, ends, own_w))

    oth, turned, grads = call(
        other_kernel,
        [((features, width), jnp.float32), ((features, rows), g.dtype), ((ny, rows, block), g.dtype)],
        [SMEM, SMEM, VMEM, VMEM, VMEM],
        "weight_grads_other",
        scratch=[pltpu.VMEM((features, rows), g.dtype)],
        flops=work,
        moved=3_000_000,
    )(lengths, jnp.stack([group, lax.axis_index("tensor")]).astype(jnp.int32), grads, ends, x)
    got = lax.ppermute(oth, "c", swap)
    (mine,) = call(
        own_kernel, [((features, width), jnp.float32)], [VMEM, VMEM], "weight_grads_own", flops=work, moved=3_000_000
    )(turned, x)

    peers = nz * nx
    (code,) = call(pack_kernel, [((peers, 8, width + lanes), jnp.int16)], [VMEM] * 2, "pack", moved=4_000_000)(
        mine.reshape(peers, 8, width), got.reshape(peers, 8, width)
    )
    code, own_w = lax.optimization_barrier((code, own_w))
    code = lax.all_to_all(code, ("z", "x"), 0, 0)
    oth_w = lax.ppermute(own_w, "c", swap)
    scale = 1.0 / math.sqrt(rows * peers * 2)
    (grad_weight,) = call(
        functools.partial(sum_kernel, scale), [((8, width), jnp.float32)], [VMEM], "unpack_sum", moved=1_000_000
    )(code)
    (grad_input,) = call(
        input_kernel,
        [((rows, width), jnp.bfloat16)],
        [VMEM] * 3,
        "input_grads",
        scratch=[pltpu.VMEM((2 * features, width), w.dtype)],
        flops=2 * work,
        moved=4_000_000,
    )(grads, own_w, oth_w)
    return (grad_input, grad_weight)


def solution(mesh):
    dp, ny = mesh.shape["dp"], mesh.shape["tensor"]
    nz, nx = ny, dp // (2 * ny)
    fine = Mesh(mesh.devices.reshape(nz, nx, 2, ny), ("z", "x", "c", "tensor"))
    both = P(("z", "x", "c"), "tensor")
    return jax.shard_map(
        functools.partial(per_device, nz, nx, ny),
        mesh=fine,
        in_specs=(both, both, both, P()),
        out_specs=(both, both),
        check_vma=False,
    )
```

```python
import functools
import math

import jax
import jax.numpy as jnp
from jax import lax
from jax.experimental import pallas as pl
from jax.experimental.pallas import tpu as pltpu
from jax.sharding import Mesh, PartitionSpec as P

STEPS = 256.0
LARGEST = 32767.0
BIAS = 127.0
VMEM = pl.BlockSpec(memory_space=pltpu.VMEM)
HBM = pl.BlockSpec(memory_space=pltpu.HBM)
SMEM = pl.BlockSpec(memory_space=pltpu.SMEM)


def sort_kernel(place_ref, lengths_ref, in_ref, out_ref, known_ref, g_ref, known_sem, g_sem):
    known = pltpu.make_async_copy(lengths_ref, known_ref, known_sem)
    grads = pltpu.make_async_copy(in_ref, g_ref, g_sem)
    known.start()
    grads.start()
    rows, width = g_ref.shape
    half = width // 2
    core = place_ref[0] % 2
    take = lax.broadcasted_iota(jnp.int32, (width, width), 0)
    place = lax.broadcasted_iota(jnp.int32, (width, width), 1)
    inner = place % half
    kind = jnp.where(place < half, core, 1 - core)
    order = jnp.where(take == (inner // 8) * 16 + inner % 8 + 8 * kind, 1.0, 0.0).astype(g_ref.dtype)
    slot = lax.broadcasted_iota(jnp.int32, (rows, width), 0)
    known.wait()
    live = slot < known_ref[place_ref[0]]
    grads.wait()
    g = jnp.dot(g_ref[...], order, preferred_element_type=jnp.float32)
    g = jnp.where(live, g, 0.0).astype(out_ref.dtype)
    for k in range(out_ref.shape[0]):
        out_ref[k] = g


def other_kernel(g_ref, x_ref, oth_ref, own_ref, turned_ref):
    blocks, rows, width = g_ref.shape
    half = width // 2
    for k in range(blocks):
        turned = g_ref[k].T
        own_ref[k * half : (k + 1) * half, :] = turned[:half]
        turned_ref[k * half : (k + 1) * half, :] = turned[half:]
    oth_ref[...] = jnp.dot(turned_ref[...], x_ref[...], preferred_element_type=jnp.float32)


def own_kernel(g_ref, x_ref, out_ref):
    out_ref[...] = jnp.dot(g_ref[...], x_ref[...], preferred_element_type=jnp.float32)


def turned_place(k, lines, line):
    return k % line * lines + k // line


def pack_kernel(line, a_ref, b_ref, w_ref, out_ref):
    rows, width = w_ref.shape
    lanes = out_ref.shape[2] - 2 * width

    def store(k, at, v):
        out_ref[k, :, at : at + v.shape[1]] = v.astype(jnp.int32).astype(out_ref.dtype)

    w = w_ref[...].astype(jnp.float32)
    size = jnp.abs(w)
    e = jnp.floor(jnp.log2(jnp.maximum(size, 2.0**-126)))
    bits = (e + BIAS) * 128.0 + (size * jnp.exp2(-e) * 128.0 - 128.0)
    bits = jnp.where(size < 2.0**-126, 0.0, bits)
    bits = jnp.round(jnp.where(w < 0.0, -bits, bits))
    for s in range(out_ref.shape[0]):
        k = turned_place(s, out_ref.shape[0] // line, line)
        v = a_ref[s] + b_ref[s]
        top = jnp.maximum(jnp.max(jnp.abs(v), axis=1, keepdims=True), 1e-30)
        e = jnp.ceil(STEPS * jnp.log2(top * (1.0 / LARGEST))) + 1.0
        store(k, 0, jnp.round(v * jnp.exp2(e * (-1.0 / STEPS))))
        store(k, width, jnp.broadcast_to(e, (rows, lanes)))
        store(k, width + lanes, bits)


def weights_kernel(line, in_ref, out_ref):
    width = out_ref.shape[2]
    for k in range(in_ref.shape[0]):
        s = turned_place(k, in_ref.shape[0] // line, line)
        bits = in_ref[s, :, in_ref.shape[2] - width :].astype(jnp.int32)
        size = jnp.abs(bits)
        e = (size >> 7).astype(jnp.float32) - BIAS
        v = ((size & 127) + 128).astype(jnp.float32) * jnp.exp2(e) * (1.0 / 128.0)
        v = jnp.where(size < 128, 0.0, jnp.where(bits < 0, -v, v))
        out_ref[k] = v.astype(out_ref.dtype)


def sum_kernel(scale, in_ref, out_ref):
    rows, width = out_ref.shape
    lanes = in_ref.shape[2] - 2 * width
    total = [jnp.zeros((rows, lanes), jnp.float32) for _ in range(width // lanes)]
    for s in range(in_ref.shape[0]):
        step = jnp.exp2(in_ref[s, :, width : width + lanes].astype(jnp.int32).astype(jnp.float32) * (1.0 / STEPS))
        for t in range(width // lanes):
            q = in_ref[s, :, t * lanes : (t + 1) * lanes].astype(jnp.int32).astype(jnp.float32)
            total[t] = total[t] + q * step
    for t in range(width // lanes):
        out_ref[:, t * lanes : (t + 1) * lanes] = total[t] * scale


def input_kernel(g_ref, own_ref, oth_ref, out_ref, w_ref, part_ref, sems):
    blocks, rows, width = g_ref.shape
    half = width // 2
    for k in range(blocks):
        w_ref[k * width : k * width + half, :] = own_ref[k * half : (k + 1) * half, :]
        w_ref[k * width + half : (k + 1) * width, :] = oth_ref[k * half : (k + 1) * half, :]
    parts = sems.shape[0]
    size = rows // parts
    copies = []
    for i in range(parts):
        at = slice(i * size, (i + 1) * size)
        g = jnp.concatenate([g_ref[k, at, :] for k in range(blocks)], axis=1)
        part_ref[at, :] = jnp.dot(g, w_ref[...], preferred_element_type=jnp.float32).astype(out_ref.dtype)
        copies.append(pltpu.make_async_copy(part_ref.at[at], out_ref.at[at], sems.at[i]))
        copies[-1].start()
    for copy in copies:
        copy.wait()


def call(kernel, out, specs, name, scratch=(), flops=0, moved=0, place=VMEM):
    return pl.pallas_call(
        kernel,
        out_shape=[jax.ShapeDtypeStruct(*o) for o in out],
        in_specs=specs,
        out_specs=[place] * len(out),
        scratch_shapes=scratch,
        compiler_params=pltpu.CompilerParams(vmem_limit_bytes=14 * 1024 * 1024),
        cost_estimate=pl.CostEstimate(flops=flops, bytes_accessed=moved, transcendentals=0),
        name=name,
    )


def per_device(nz, nx, ny, x, g, w, lengths):
    rows, width = x.shape
    block = g.shape[1]
    half = block // 2
    features = ny * half
    lanes = 128
    work = 2 * rows * features * width
    group = (lax.axis_index("z") * nx + lax.axis_index("x")) * 2 + lax.axis_index("c")
    swap = [(0, 1), (1, 0)]

    (copies,) = call(
        sort_kernel,
        [((ny, rows, block), g.dtype)],
        [SMEM, HBM, HBM],
        "sort",
        scratch=[
            pltpu.SMEM(lengths.shape, lengths.dtype),
            pltpu.VMEM((rows, block), g.dtype),
            pltpu.SemaphoreType.DMA,
            pltpu.SemaphoreType.DMA,
        ],
        moved=2_000_000,
    )(group.astype(jnp.int32).reshape(1), lengths, g)
    grads = lax.all_to_all(copies, "tensor", 0, 0)

    oth, turned = call(
        other_kernel,
        [((features, width), jnp.float32), ((features, rows), g.dtype)],
        [VMEM, VMEM],
        "weight_grads_other",
        scratch=[pltpu.VMEM((features, rows), g.dtype)],
        flops=work,
        moved=3_000_000,
    )(grads, x)
    got = lax.ppermute(oth, "c", swap)
    (mine,) = call(
        own_kernel, [((features, width), jnp.float32)], [VMEM, VMEM], "weight_grads_own", flops=work, moved=3_000_000
    )(turned, x)

    peers = nz * nx
    (code,) = call(functools.partial(pack_kernel, nx), [((peers, 8, 2 * width + lanes), jnp.int16)], [VMEM] * 3, "pack", moved=4_000_000)(
        mine.reshape(peers, 8, width), got.reshape(peers, 8, width), w
    )
    code = lax.all_to_all(code, ("x", "z"), 0, 0)
    (own_w,) = call(functools.partial(weights_kernel, nx), [((peers, 8, width), w.dtype)], [VMEM], "unpack_weights", moved=1_500_000)(code)
    own_w = own_w.reshape(features, width)
    oth_w = lax.ppermute(own_w, "c", swap)
    scale = 1.0 / math.sqrt(rows * peers * 2)
    (grad_weight,) = call(
        functools.partial(sum_kernel, scale), [((8, width), jnp.float32)], [VMEM], "unpack_sum", moved=1_000_000
    )(code)
    (grad_input,) = call(
        input_kernel,
        [((rows, width), jnp.bfloat16)],
        [VMEM] * 3,
        "input_grads",
        scratch=[
            pltpu.VMEM((2 * features, width), w.dtype),
            pltpu.VMEM((rows, width), w.dtype),
            pltpu.SemaphoreType.DMA((2,)),
        ],
        flops=2 * work,
        moved=4_000_000,
        place=HBM,
    )(grads, own_w, oth_w)
    return (grad_input, grad_weight)


def solution(mesh):
    dp, ny = mesh.shape["dp"], mesh.shape["tensor"]
    nz, nx = ny, dp // (2 * ny)
    fine = Mesh(mesh.devices.reshape(nz, nx, 2, ny), ("z", "x", "c", "tensor"))
    both = P(("z", "x", "c"), "tensor")
    return jax.shard_map(
        functools.partial(per_device, nz, nx, ny),
        mesh=fine,
        in_specs=(both, both, both, P()),
        out_specs=(both, both),
        check_vma=False,
    )
```

```python
import functools
import math

import jax
import jax.numpy as jnp
from jax import lax
from jax.experimental import pallas as pl
from jax.experimental.pallas import tpu as pltpu
from jax.sharding import Mesh, PartitionSpec as P

STEPS = 256.0
LARGEST = 32767.0
BIAS = 127.0
VMEM = pl.BlockSpec(memory_space=pltpu.VMEM)
SMEM = pl.BlockSpec(memory_space=pltpu.SMEM)


def sort_kernel(place_ref, g_ref, out_ref):
    width = g_ref.shape[1]
    half = width // 2
    core = place_ref[0] % 2
    take = lax.broadcasted_iota(jnp.int32, (width, width), 0)
    place = lax.broadcasted_iota(jnp.int32, (width, width), 1)
    inner = place % half
    kind = jnp.where(place < half, core, 1 - core)
    order = jnp.where(take == (inner // 8) * 16 + inner % 8 + 8 * kind, 1.0, 0.0).astype(g_ref.dtype)
    g = jnp.dot(g_ref[...], order, preferred_element_type=jnp.float32).astype(out_ref.dtype)
    for k in range(out_ref.shape[0]):
        out_ref[k] = g


def other_kernel(lengths_ref, place_ref, g_ref, x_ref, sum_ref, own_ref, oth_ref, live_ref):
    blocks, rows, width = g_ref.shape
    half = width // 2
    live = lax.broadcasted_iota(jnp.int32, x_ref.shape, 0) < lengths_ref[place_ref[0]]
    live_ref[...] = jnp.where(live, x_ref[...].astype(jnp.float32), 0.0).astype(x_ref.dtype)
    for k in range(blocks):
        turned = g_ref[k].T
        own_ref[k * half : (k + 1) * half, :] = turned[:half]
        oth_ref[k * half : (k + 1) * half, :] = turned[half:]
    sum_ref[...] = jnp.dot(oth_ref[...], live_ref[...], preferred_element_type=jnp.float32)


def own_kernel(g_ref, x_ref, out_ref):
    out_ref[...] = jnp.dot(g_ref[...], x_ref[...], preferred_element_type=jnp.float32)


def turned_place(k, lines, line):
    return k % line * lines + k // line


def pack_kernel(line, a_ref, b_ref, w_ref, out_ref):
    rows, width = w_ref.shape
    lanes = out_ref.shape[2] - 2 * width

    def store(k, at, v):
        out_ref[k, :, at : at + v.shape[1]] = v.astype(jnp.int32).astype(out_ref.dtype)

    w = w_ref[...].astype(jnp.float32)
    size = jnp.abs(w)
    e = jnp.floor(jnp.log2(jnp.maximum(size, 2.0**-126)))
    bits = (e + BIAS) * 128.0 + (size * jnp.exp2(-e) * 128.0 - 128.0)
    bits = jnp.where(size < 2.0**-126, 0.0, bits)
    bits = jnp.round(jnp.where(w < 0.0, -bits, bits))
    for s in range(out_ref.shape[0]):
        k = turned_place(s, out_ref.shape[0] // line, line)
        v = a_ref[s] + b_ref[s]
        top = jnp.maximum(jnp.max(jnp.abs(v), axis=1, keepdims=True), 1e-30)
        e = jnp.ceil(STEPS * jnp.log2(top * (1.0 / LARGEST))) + 1.0
        store(k, 0, jnp.round(v * jnp.exp2(e * (-1.0 / STEPS))))
        store(k, width, jnp.broadcast_to(e, (rows, lanes)))
        store(k, width + lanes, bits)


def weights_kernel(line, in_ref, out_ref):
    width = out_ref.shape[2]
    for k in range(in_ref.shape[0]):
        s = turned_place(k, in_ref.shape[0] // line, line)
        bits = in_ref[s, :, in_ref.shape[2] - width :].astype(jnp.int32)
        size = jnp.abs(bits)
        e = (size >> 7).astype(jnp.float32) - BIAS
        v = ((size & 127) + 128).astype(jnp.float32) * jnp.exp2(e) * (1.0 / 128.0)
        v = jnp.where(size < 128, 0.0, jnp.where(bits < 0, -v, v))
        out_ref[k] = v.astype(out_ref.dtype)


def sum_kernel(scale, in_ref, out_ref):
    rows, width = out_ref.shape
    lanes = in_ref.shape[2] - 2 * width
    total = [jnp.zeros((rows, lanes), jnp.float32) for _ in range(width // lanes)]
    for s in range(in_ref.shape[0]):
        step = jnp.exp2(in_ref[s, :, width : width + lanes].astype(jnp.int32).astype(jnp.float32) * (1.0 / STEPS))
        for t in range(width // lanes):
            q = in_ref[s, :, t * lanes : (t + 1) * lanes].astype(jnp.int32).astype(jnp.float32)
            total[t] = total[t] + q * step
    for t in range(width // lanes):
        out_ref[:, t * lanes : (t + 1) * lanes] = total[t] * scale


def turned_dot(g, w):
    return lax.dot_general(g, w, (((0,), (0,)), ((), ())), preferred_element_type=jnp.float32)


def first_kernel(g_ref, w_ref, out_ref):
    out_ref[...] = turned_dot(g_ref[...], w_ref[...])


def input_kernel(lengths_ref, place_ref, part_ref, g_ref, w_ref, out_ref):
    live = lax.broadcasted_iota(jnp.int32, out_ref.shape, 0) < lengths_ref[place_ref[0]]
    total = part_ref[...] + turned_dot(g_ref[...], w_ref[...])
    out_ref[...] = jnp.where(live, total, 0.0).astype(out_ref.dtype)


def call(kernel, out, specs, name, scratch=(), flops=0, moved=0):
    return pl.pallas_call(
        kernel,
        out_shape=[jax.ShapeDtypeStruct(*o) for o in out],
        in_specs=specs,
        out_specs=[VMEM] * len(out),
        scratch_shapes=scratch,
        compiler_params=pltpu.CompilerParams(vmem_limit_bytes=14 * 1024 * 1024),
        cost_estimate=pl.CostEstimate(flops=flops, bytes_accessed=moved, transcendentals=0),
        name=name,
    )


def per_device(nz, nx, ny, x, g, w, lengths):
    rows, width = x.shape
    block = g.shape[1]
    half = block // 2
    features = ny * half
    lanes = 128
    work = 2 * rows * features * width
    group = (lax.axis_index("z") * nx + lax.axis_index("x")) * 2 + lax.axis_index("c")
    swap = [(0, 1), (1, 0)]

    place = group.astype(jnp.int32).reshape(1)
    (copies,) = call(sort_kernel, [((ny, rows, block), g.dtype)], [SMEM, VMEM], "sort", moved=2_000_000)(place, g)
    grads = lax.all_to_all(copies, "tensor", 0, 0)

    turned = ((features, rows), g.dtype)
    oth, own_g, oth_g, live_x = call(
        other_kernel,
        [((features, width), jnp.float32), turned, turned, (x.shape, x.dtype)],
        [SMEM, SMEM, VMEM, VMEM],
        "weight_grads_other",
        flops=work,
        moved=3_000_000,
    )(lengths, place, grads, x)
    got = lax.ppermute(oth, "c", swap)
    (mine,) = call(
        own_kernel, [((features, width), jnp.float32)], [VMEM, VMEM], "weight_grads_own", flops=work, moved=3_000_000
    )(own_g, live_x)

    peers = nz * nx
    (code,) = call(functools.partial(pack_kernel, nx), [((peers, 8, 2 * width + lanes), jnp.int16)], [VMEM] * 3, "pack", moved=4_000_000)(
        mine.reshape(peers, 8, width), got.reshape(peers, 8, width), w
    )
    code = lax.all_to_all(code, ("x", "z"), 0, 0)
    (own_w,) = call(functools.partial(weights_kernel, nx), [((peers, 8, width), w.dtype)], [VMEM], "unpack_weights", moved=1_500_000)(code)
    own_w = own_w.reshape(features, width)
    oth_w = lax.ppermute(own_w, "c", swap)
    scale = 1.0 / math.sqrt(rows * peers * 2)
    (grad_weight,) = call(
        functools.partial(sum_kernel, scale), [((8, width), jnp.float32)], [VMEM], "unpack_sum", moved=1_000_000
    )(code)
    (part,) = call(
        first_kernel, [((rows, width), jnp.float32)], [VMEM] * 2, "input_grads_own", flops=work, moved=3_000_000
    )(own_g, own_w)
    (grad_input,) = call(
        input_kernel,
        [((rows, width), jnp.bfloat16)],
        [SMEM, SMEM, VMEM, VMEM, VMEM],
        "input_grads",
        flops=work,
        moved=4_000_000,
    )(lengths, place, part, oth_g, oth_w)
    return (grad_input, grad_weight)


def solution(mesh):
    dp, ny = mesh.shape["dp"], mesh.shape["tensor"]
    nz, nx = ny, dp // (2 * ny)
    fine = Mesh(mesh.devices.reshape(nz, nx, 2, ny), ("z", "x", "c", "tensor"))
    both = P(("z", "x", "c"), "tensor")
    return jax.shard_map(
        functools.partial(per_device, nz, nx, ny),
        mesh=fine,
        in_specs=(both, both, both, P()),
        out_specs=(both, both),
        check_vma=False,
    )
```

```python
import functools
import math

import jax
import jax.numpy as jnp
from jax import lax
from jax.experimental import pallas as pl
from jax.experimental.pallas import tpu as pltpu
from jax.sharding import Mesh, PartitionSpec as P

STEPS = 256.0
LARGEST = 32767.0
BIAS = 127.0
VMEM = pl.BlockSpec(memory_space=pltpu.VMEM)
HBM = pl.BlockSpec(memory_space=pltpu.HBM)
SMEM = pl.BlockSpec(memory_space=pltpu.SMEM)


def sort_kernel(place_ref, g_ref, out_ref):
    width = g_ref.shape[1]
    half = width // 2
    core = place_ref[0] % 2
    take = lax.broadcasted_iota(jnp.int32, (width, width), 0)
    place = lax.broadcasted_iota(jnp.int32, (width, width), 1)
    inner = place % half
    kind = jnp.where(place < half, core, 1 - core)
    order = jnp.where(take == (inner // 8) * 16 + inner % 8 + 8 * kind, 1.0, 0.0).astype(g_ref.dtype)
    g = jnp.dot(g_ref[...], order, preferred_element_type=jnp.float32).astype(out_ref.dtype)
    for k in range(out_ref.shape[0]):
        out_ref[k] = g


def other_kernel(lengths_ref, place_ref, g_ref, x_ref, sum_ref, own_ref, oth_ref, live_ref):
    blocks, rows, width = g_ref.shape
    half = width // 2
    live = lax.broadcasted_iota(jnp.int32, x_ref.shape, 0) < lengths_ref[place_ref[0]]
    live_ref[...] = jnp.where(live, x_ref[...].astype(jnp.float32), 0.0).astype(x_ref.dtype)
    for k in range(blocks):
        turned = g_ref[k].T
        own_ref[k * half : (k + 1) * half, :] = turned[:half]
        oth_ref[k * half : (k + 1) * half, :] = turned[half:]
    sum_ref[...] = jnp.dot(oth_ref[...], live_ref[...], preferred_element_type=jnp.float32)


def own_kernel(own_ref, oth_ref, x_ref, sum_ref, own_back_ref, oth_back_ref):
    sum_ref[...] = jnp.dot(own_ref[...], x_ref[...], preferred_element_type=jnp.float32)
    own_back_ref[...] = own_ref[...].T
    oth_back_ref[...] = oth_ref[...].T


def turned_place(k, lines, line):
    return k % line * lines + k // line


def pack_kernel(line, a_ref, b_ref, w_ref, out_ref):
    rows, width = w_ref.shape
    lanes = out_ref.shape[2] - 2 * width

    def store(k, at, v):
        out_ref[k, :, at : at + v.shape[1]] = v.astype(jnp.int32).astype(out_ref.dtype)

    w = w_ref[...].astype(jnp.float32)
    size = jnp.abs(w)
    e = jnp.floor(jnp.log2(jnp.maximum(size, 2.0**-126)))
    bits = (e + BIAS) * 128.0 + (size * jnp.exp2(-e) * 128.0 - 128.0)
    bits = jnp.where(size < 2.0**-126, 0.0, bits)
    bits = jnp.round(jnp.where(w < 0.0, -bits, bits))
    for s in range(out_ref.shape[0]):
        k = turned_place(s, out_ref.shape[0] // line, line)
        v = a_ref[s] + b_ref[s]
        top = jnp.maximum(jnp.max(jnp.abs(v), axis=1, keepdims=True), 1e-30)
        e = jnp.ceil(STEPS * jnp.log2(top * (1.0 / LARGEST))) + 1.0
        store(k, 0, jnp.round(v * jnp.exp2(e * (-1.0 / STEPS))))
        store(k, width, jnp.broadcast_to(e, (rows, lanes)))
        store(k, width + lanes, bits)


def weights_kernel(line, in_ref, out_ref):
    width = out_ref.shape[2]
    for k in range(in_ref.shape[0]):
        s = turned_place(k, in_ref.shape[0] // line, line)
        bits = in_ref[s, :, in_ref.shape[2] - width :].astype(jnp.int32)
        size = jnp.abs(bits)
        e = (size >> 7).astype(jnp.float32) - BIAS
        v = ((size & 127) + 128).astype(jnp.float32) * jnp.exp2(e) * (1.0 / 128.0)
        v = jnp.where(size < 128, 0.0, jnp.where(bits < 0, -v, v))
        out_ref[k] = v.astype(out_ref.dtype)


def sum_kernel(scale, in_ref, out_ref):
    rows, width = out_ref.shape
    lanes = in_ref.shape[2] - 2 * width
    total = [jnp.zeros((rows, lanes), jnp.float32) for _ in range(width // lanes)]
    for s in range(in_ref.shape[0]):
        step = jnp.exp2(in_ref[s, :, width : width + lanes].astype(jnp.int32).astype(jnp.float32) * (1.0 / STEPS))
        for t in range(width // lanes):
            q = in_ref[s, :, t * lanes : (t + 1) * lanes].astype(jnp.int32).astype(jnp.float32)
            total[t] = total[t] + q * step
    for t in range(width // lanes):
        out_ref[:, t * lanes : (t + 1) * lanes] = total[t] * scale


def first_kernel(g_ref, w_ref, out_ref):
    out_ref[...] = jnp.dot(g_ref[...], w_ref[...], preferred_element_type=jnp.float32)


def input_kernel(lengths_ref, place_ref, part_ref, g_ref, w_ref, out_ref, held_ref, sems):
    length = lengths_ref[place_ref[0]]
    size = out_ref.shape[0] // sems.shape[0]
    copies = []
    for i in range(sems.shape[0]):
        at = slice(i * size, (i + 1) * size)
        total = part_ref[at, :] + jnp.dot(g_ref[at, :], w_ref[...], preferred_element_type=jnp.float32)
        live = lax.broadcasted_iota(jnp.int32, total.shape, 0) + i * size < length
        held_ref[at, :] = jnp.where(live, total, 0.0).astype(out_ref.dtype)
        copies.append(pltpu.make_async_copy(held_ref.at[at], out_ref.at[at], sems.at[i]))
        copies[-1].start()
    for copy in copies:
        copy.wait()


def call(kernel, out, specs, name, scratch=(), flops=0, moved=0, place=VMEM):
    return pl.pallas_call(
        kernel,
        out_shape=[jax.ShapeDtypeStruct(*o) for o in out],
        in_specs=specs,
        out_specs=[place] * len(out),
        scratch_shapes=scratch,
        compiler_params=pltpu.CompilerParams(vmem_limit_bytes=14 * 1024 * 1024),
        cost_estimate=pl.CostEstimate(flops=flops, bytes_accessed=moved, transcendentals=0),
        name=name,
    )


def per_device(nz, nx, ny, x, g, w, lengths):
    rows, width = x.shape
    block = g.shape[1]
    half = block // 2
    features = ny * half
    lanes = 128
    work = 2 * rows * features * width
    group = (lax.axis_index("z") * nx + lax.axis_index("x")) * 2 + lax.axis_index("c")
    swap = [(0, 1), (1, 0)]

    place = group.astype(jnp.int32).reshape(1)
    (copies,) = call(sort_kernel, [((ny, rows, block), g.dtype)], [SMEM, VMEM], "sort", moved=2_000_000)(place, g)
    grads = lax.all_to_all(copies, "tensor", 0, 0)

    turned = ((features, rows), g.dtype)
    oth, own_g, oth_g, live_x = call(
        other_kernel,
        [((features, width), jnp.float32), turned, turned, (x.shape, x.dtype)],
        [SMEM, SMEM, VMEM, VMEM],
        "weight_grads_other",
        flops=work,
        moved=3_000_000,
    )(lengths, place, grads, x)
    got = lax.ppermute(oth, "c", swap)
    back = ((rows, features), g.dtype)
    mine, own_g, oth_g = call(
        own_kernel,
        [((features, width), jnp.float32), back, back],
        [VMEM] * 3,
        "weight_grads_own",
        flops=work,
        moved=3_000_000,
    )(own_g, oth_g, live_x)

    peers = nz * nx
    (code,) = call(functools.partial(pack_kernel, nx), [((peers, 8, 2 * width + lanes), jnp.int16)], [VMEM] * 3, "pack", moved=4_000_000)(
        mine.reshape(peers, 8, width), got.reshape(peers, 8, width), w
    )
    code = lax.all_to_all(code, ("x", "z"), 0, 0)
    (own_w,) = call(functools.partial(weights_kernel, nx), [((peers, 8, width), w.dtype)], [VMEM], "unpack_weights", moved=1_500_000)(code)
    own_w = own_w.reshape(features, width)
    oth_w = lax.ppermute(own_w, "c", swap)
    scale = 1.0 / math.sqrt(rows * peers * 2)
    (grad_weight,) = call(
        functools.partial(sum_kernel, scale), [((8, width), jnp.float32)], [VMEM], "unpack_sum", moved=1_000_000
    )(code)
    (part,) = call(
        first_kernel, [((rows, width), jnp.float32)], [VMEM] * 2, "input_grads_own", flops=work, moved=3_000_000
    )(own_g, own_w)
    (grad_input,) = call(
        input_kernel,
        [((rows, width), jnp.bfloat16)],
        [SMEM, SMEM, VMEM, VMEM, VMEM],
        "input_grads",
        scratch=[pltpu.VMEM((rows, width), w.dtype), pltpu.SemaphoreType.DMA((4,))],
        flops=work,
        moved=4_000_000,
        place=HBM,
    )(lengths, place, part, oth_g, oth_w)
    return (grad_input, grad_weight)


def solution(mesh):
    dp, ny = mesh.shape["dp"], mesh.shape["tensor"]
    nz, nx = ny, dp // (2 * ny)
    fine = Mesh(mesh.devices.reshape(nz, nx, 2, ny), ("z", "x", "c", "tensor"))
    both = P(("z", "x", "c"), "tensor")
    return jax.shard_map(
        functools.partial(per_device, nz, nx, ny),
        mesh=fine,
        in_specs=(both, both, both, P()),
        out_specs=(both, both),
        check_vma=False,
    )
```

```python
import functools
import math

import jax
import jax.numpy as jnp
from jax import lax
from jax.experimental import pallas as pl
from jax.experimental.pallas import tpu as pltpu
from jax.sharding import Mesh, PartitionSpec as P

STEPS = 256.0
LARGEST = 32767.0
BIAS = 127.0
VMEM = pl.BlockSpec(memory_space=pltpu.VMEM)
HBM = pl.BlockSpec(memory_space=pltpu.HBM)
SMEM = pl.BlockSpec(memory_space=pltpu.SMEM)


def sort_kernel(place_ref, g_ref, out_ref):
    width = g_ref.shape[1]
    half = width // 2
    core = place_ref[0] % 2
    take = lax.broadcasted_iota(jnp.int32, (width, width), 0)
    place = lax.broadcasted_iota(jnp.int32, (width, width), 1)
    inner = place % half
    kind = jnp.where(place < half, core, 1 - core)
    order = jnp.where(take == (inner // 8) * 16 + inner % 8 + 8 * kind, 1.0, 0.0).astype(g_ref.dtype)
    g = jnp.dot(g_ref[...], order, preferred_element_type=jnp.float32).astype(out_ref.dtype)
    for k in range(out_ref.shape[0]):
        out_ref[k] = g


def other_kernel(lengths_ref, place_ref, g_ref, x_ref, sum_ref, own_ref, oth_ref, live_ref):
    blocks, rows, width = g_ref.shape
    half = width // 2
    live = lax.broadcasted_iota(jnp.int32, x_ref.shape, 0) < lengths_ref[place_ref[0]]
    live_ref[...] = jnp.where(live, x_ref[...].astype(jnp.float32), 0.0).astype(x_ref.dtype)
    for k in range(blocks):
        turned = g_ref[k].T
        own_ref[k * half : (k + 1) * half, :] = turned[:half]
        oth_ref[k * half : (k + 1) * half, :] = turned[half:]
    sum_ref[...] = jnp.dot(oth_ref[...], live_ref[...], preferred_element_type=jnp.float32)


def own_kernel(own_ref, oth_ref, x_ref, sum_ref, own_back_ref, oth_back_ref):
    sum_ref[...] = jnp.dot(own_ref[...], x_ref[...], preferred_element_type=jnp.float32)
    own_back_ref[...] = own_ref[...].T
    oth_back_ref[...] = oth_ref[...].T


def turned_place(k, lines, line):
    return k % line * lines + k // line


def pack_kernel(line, a_ref, b_ref, w_ref, out_ref):
    rows, width = w_ref.shape
    lanes = out_ref.shape[2] - 2 * width

    def store(k, at, v):
        out_ref[k, :, at : at + v.shape[1]] = v.astype(jnp.int32).astype(out_ref.dtype)

    w = w_ref[...].astype(jnp.float32)
    size = jnp.abs(w)
    e = jnp.floor(jnp.log2(jnp.maximum(size, 2.0**-126)))
    bits = (e + BIAS) * 128.0 + (size * jnp.exp2(-e) * 128.0 - 128.0)
    bits = jnp.where(size < 2.0**-126, 0.0, bits)
    bits = jnp.round(jnp.where(w < 0.0, -bits, bits))
    for s in range(out_ref.shape[0]):
        k = turned_place(s, out_ref.shape[0] // line, line)
        v = a_ref[s] + b_ref[s]
        top = jnp.maximum(jnp.max(jnp.abs(v), axis=1, keepdims=True), 1e-30)
        e = jnp.ceil(STEPS * jnp.log2(top * (1.0 / LARGEST))) + 1.0
        store(k, 0, jnp.round(v * jnp.exp2(e * (-1.0 / STEPS))))
        store(k, width, jnp.broadcast_to(e, (rows, lanes)))
        store(k, width + lanes, bits)


def weights_kernel(line, in_ref, out_ref):
    width = out_ref.shape[2]
    for k in range(in_ref.shape[0]):
        s = turned_place(k, in_ref.shape[0] // line, line)
        bits = in_ref[s, :, in_ref.shape[2] - width :].astype(jnp.int32)
        size = jnp.abs(bits)
        e = (size >> 7).astype(jnp.float32) - BIAS
        v = ((size & 127) + 128).astype(jnp.float32) * jnp.exp2(e) * (1.0 / 128.0)
        v = jnp.where(size < 128, 0.0, jnp.where(bits < 0, -v, v))
        out_ref[k] = v.astype(out_ref.dtype)


def sum_kernel(scale, in_ref, out_ref):
    rows, width = out_ref.shape
    lanes = in_ref.shape[2] - 2 * width
    total = [jnp.zeros((rows, lanes), jnp.float32) for _ in range(width // lanes)]
    for s in range(in_ref.shape[0]):
        step = jnp.exp2(in_ref[s, :, width : width + lanes].astype(jnp.int32).astype(jnp.float32) * (1.0 / STEPS))
        for t in range(width // lanes):
            q = in_ref[s, :, t * lanes : (t + 1) * lanes].astype(jnp.int32).astype(jnp.float32)
            total[t] = total[t] + q * step
    for t in range(width // lanes):
        out_ref[:, t * lanes : (t + 1) * lanes] = total[t] * scale


def first_kernel(g_ref, w_ref, out_ref):
    out_ref[...] = jnp.dot(g_ref[...], w_ref[...], preferred_element_type=jnp.float32)


def input_kernel(lengths_ref, place_ref, part_ref, g_ref, w_ref, out_ref, held_ref, sems):
    length = lengths_ref[place_ref[0]]
    size = out_ref.shape[0] // sems.shape[0]
    copies = []
    for i in range(sems.shape[0]):
        at = slice(i * size, (i + 1) * size)
        total = part_ref[at, :] + jnp.dot(g_ref[at, :], w_ref[...], preferred_element_type=jnp.float32)
        live = lax.broadcasted_iota(jnp.int32, total.shape, 0) + i * size < length
        held_ref[at, :] = jnp.where(live, total, 0.0).astype(out_ref.dtype)
        copies.append(pltpu.make_async_copy(held_ref.at[at], out_ref.at[at], sems.at[i]))
        copies[-1].start()
    for copy in copies:
        copy.wait()


def call(kernel, out, specs, name, scratch=(), flops=0, moved=0, place=VMEM):
    return pl.pallas_call(
        kernel,
        out_shape=[jax.ShapeDtypeStruct(*o) for o in out],
        in_specs=specs,
        out_specs=[place] * len(out),
        scratch_shapes=scratch,
        compiler_params=pltpu.CompilerParams(vmem_limit_bytes=14 * 1024 * 1024),
        cost_estimate=pl.CostEstimate(flops=flops, bytes_accessed=moved, transcendentals=0),
        name=name,
    )


def per_device(nz, nx, ny, x, g, w, lengths):
    rows, width = x.shape
    block = g.shape[1]
    half = block // 2
    features = ny * half
    lanes = 128
    work = 2 * rows * features * width
    group = (lax.axis_index("z") * nx + lax.axis_index("x")) * 2 + lax.axis_index("c")
    swap = [(0, 1), (1, 0)]

    place = group.astype(jnp.int32).reshape(1)
    (copies,) = call(sort_kernel, [((ny, rows, block), g.dtype)], [SMEM, VMEM], "sort", moved=2_000_000)(place, g)
    grads = lax.all_to_all(copies, "tensor", 0, 0)

    turned = ((features, rows), g.dtype)
    oth, own_g, oth_g, live_x = call(
        other_kernel,
        [((features, width), jnp.float32), turned, turned, (x.shape, x.dtype)],
        [SMEM, SMEM, VMEM, VMEM],
        "weight_grads_other",
        flops=work,
        moved=3_000_000,
    )(lengths, place, grads, x)
    got = lax.ppermute(oth, "c", swap)
    back = ((rows, features), g.dtype)
    mine, own_g, oth_g = call(
        own_kernel,
        [((features, width), jnp.float32), back, back],
        [VMEM] * 3,
        "weight_grads_own",
        flops=work,
        moved=3_000_000,
    )(own_g, oth_g, live_x)

    peers = nz * nx
    (code,) = call(functools.partial(pack_kernel, nx), [((peers, 8, 2 * width + lanes), jnp.int16)], [VMEM] * 3, "pack", moved=4_000_000)(
        mine.reshape(peers, 8, width), got.reshape(peers, 8, width), w
    )
    code = lax.all_to_all(code, ("x", "z"), 0, 0)
    (own_w,) = call(functools.partial(weights_kernel, nx), [((peers, 8, width), w.dtype)], [VMEM], "unpack_weights", moved=1_500_000)(code)
    own_w = own_w.reshape(features, width)
    oth_w = lax.ppermute(own_w, "c", swap)
    scale = 1.0 / math.sqrt(rows * peers * 2)
    (grad_weight,) = call(
        functools.partial(sum_kernel, scale), [((8, width), jnp.float32)], [VMEM], "unpack_sum", moved=1_000_000
    )(code)
    (part,) = call(
        first_kernel, [((rows, width), jnp.float32)], [VMEM] * 2, "input_grads_own", flops=work, moved=3_000_000
    )(own_g, own_w)
    (grad_input,) = call(
        input_kernel,
        [((rows, width), jnp.bfloat16)],
        [SMEM, SMEM, VMEM, VMEM, VMEM],
        "input_grads",
        scratch=[pltpu.VMEM((rows, width), w.dtype), pltpu.SemaphoreType.DMA((2,))],
        flops=work,
        moved=4_000_000,
        place=HBM,
    )(lengths, place, part, oth_g, oth_w)
    return (grad_input, grad_weight)


def solution(mesh):
    dp, ny = mesh.shape["dp"], mesh.shape["tensor"]
    nz, nx = ny, dp // (2 * ny)
    fine = Mesh(mesh.devices.reshape(nz, nx, 2, ny), ("z", "x", "c", "tensor"))
    both = P(("z", "x", "c"), "tensor")
    return jax.shard_map(
        functools.partial(per_device, nz, nx, ny),
        mesh=fine,
        in_specs=(both, both, both, P()),
        out_specs=(both, both),
        check_vma=False,
    )
```

```python
import functools
import math

import jax
import jax.numpy as jnp
from jax import lax
from jax.experimental import pallas as pl
from jax.experimental.pallas import tpu as pltpu
from jax.sharding import Mesh, PartitionSpec as P

STEPS = 256.0
LARGEST = 32767.0
BIAS = 127.0
VMEM = pl.BlockSpec(memory_space=pltpu.VMEM)
HBM = pl.BlockSpec(memory_space=pltpu.HBM)
SMEM = pl.BlockSpec(memory_space=pltpu.SMEM)


def sort_kernel(place_ref, g_ref, out_ref):
    width = g_ref.shape[1]
    half = width // 2
    core = place_ref[0] % 2
    take = lax.broadcasted_iota(jnp.int32, (width, width), 0)
    place = lax.broadcasted_iota(jnp.int32, (width, width), 1)
    inner = place % half
    kind = jnp.where(place < half, core, 1 - core)
    order = jnp.where(take == (inner // 8) * 16 + inner % 8 + 8 * kind, 1.0, 0.0).astype(g_ref.dtype)
    g = jnp.dot(g_ref[...], order, preferred_element_type=jnp.float32).astype(out_ref.dtype)
    for k in range(out_ref.shape[0]):
        out_ref[k] = g


def other_kernel(lengths_ref, place_ref, g_ref, x_ref, sum_ref, own_ref, oth_ref, live_ref):
    blocks, rows, width = g_ref.shape
    half = width // 2
    live = lax.broadcasted_iota(jnp.int32, x_ref.shape, 0) < lengths_ref[place_ref[0]]
    live_ref[...] = jnp.where(live, x_ref[...].astype(jnp.float32), 0.0).astype(x_ref.dtype)
    for k in range(blocks):
        turned = g_ref[k].T
        own_ref[k * half : (k + 1) * half, :] = turned[:half]
        oth_ref[k * half : (k + 1) * half, :] = turned[half:]
    sum_ref[...] = jnp.dot(oth_ref[...], live_ref[...], preferred_element_type=jnp.float32)


def own_kernel(lengths_ref, place_ref, own_ref, oth_ref, x_ref, sum_ref, own_back_ref, oth_back_ref):
    sum_ref[...] = jnp.dot(own_ref[...], x_ref[...], preferred_element_type=jnp.float32)
    live = lax.broadcasted_iota(jnp.int32, own_back_ref.shape, 0) < lengths_ref[place_ref[0]]
    own_back_ref[...] = jnp.where(live, own_ref[...].T.astype(jnp.float32), 0.0).astype(own_back_ref.dtype)
    oth_back_ref[...] = jnp.where(live, oth_ref[...].T.astype(jnp.float32), 0.0).astype(oth_back_ref.dtype)


def turned_place(k, lines, line):
    return k % line * lines + k // line


def pack_kernel(line, a_ref, b_ref, w_ref, out_ref):
    rows, width = w_ref.shape
    lanes = out_ref.shape[2] - 2 * width

    def store(k, at, v):
        out_ref[k, :, at : at + v.shape[1]] = v.astype(jnp.int32).astype(out_ref.dtype)

    w = w_ref[...].astype(jnp.float32)
    size = jnp.abs(w)
    e = jnp.floor(jnp.log2(jnp.maximum(size, 2.0**-126)))
    bits = (e + BIAS) * 128.0 + (size * jnp.exp2(-e) * 128.0 - 128.0)
    bits = jnp.where(size < 2.0**-126, 0.0, bits)
    bits = jnp.round(jnp.where(w < 0.0, -bits, bits))
    for s in range(out_ref.shape[0]):
        k = turned_place(s, out_ref.shape[0] // line, line)
        v = a_ref[s] + b_ref[s]
        top = jnp.maximum(jnp.max(jnp.abs(v), axis=1, keepdims=True), 1e-30)
        e = jnp.ceil(STEPS * jnp.log2(top * (1.0 / LARGEST))) + 1.0
        store(k, 0, jnp.round(v * jnp.exp2(e * (-1.0 / STEPS))))
        store(k, width, jnp.broadcast_to(e, (rows, lanes)))
        store(k, width + lanes, bits)


def weights_kernel(line, in_ref, out_ref):
    width = out_ref.shape[2]
    for k in range(in_ref.shape[0]):
        s = turned_place(k, in_ref.shape[0] // line, line)
        bits = in_ref[s, :, in_ref.shape[2] - width :].astype(jnp.int32)
        size = jnp.abs(bits)
        e = (size >> 7).astype(jnp.float32) - BIAS
        v = ((size & 127) + 128).astype(jnp.float32) * jnp.exp2(e) * (1.0 / 128.0)
        v = jnp.where(size < 128, 0.0, jnp.where(bits < 0, -v, v))
        out_ref[k] = v.astype(out_ref.dtype)


def sum_kernel(scale, in_ref, out_ref):
    rows, width = out_ref.shape
    lanes = in_ref.shape[2] - 2 * width
    total = [jnp.zeros((rows, lanes), jnp.float32) for _ in range(width // lanes)]
    for s in range(in_ref.shape[0]):
        step = jnp.exp2(in_ref[s, :, width : width + lanes].astype(jnp.int32).astype(jnp.float32) * (1.0 / STEPS))
        for t in range(width // lanes):
            q = in_ref[s, :, t * lanes : (t + 1) * lanes].astype(jnp.int32).astype(jnp.float32)
            total[t] = total[t] + q * step
    for t in range(width // lanes):
        out_ref[:, t * lanes : (t + 1) * lanes] = total[t] * scale


def first_kernel(g_ref, w_ref, out_ref):
    out_ref[...] = jnp.dot(g_ref[...], w_ref[...], preferred_element_type=jnp.float32)


def input_kernel(part_ref, g_ref, w_ref, out_ref, held_ref, sems):
    size = out_ref.shape[0] // sems.shape[0]
    copies = []
    for i in range(sems.shape[0]):
        at = slice(i * size, (i + 1) * size)
        total = part_ref[at, :] + jnp.dot(g_ref[at, :], w_ref[...], preferred_element_type=jnp.float32)
        held_ref[at, :] = total.astype(out_ref.dtype)
        copies.append(pltpu.make_async_copy(held_ref.at[at], out_ref.at[at], sems.at[i]))
        copies[-1].start()
    for copy in copies:
        copy.wait()


def call(kernel, out, specs, name, scratch=(), flops=0, moved=0, place=VMEM):
    return pl.pallas_call(
        kernel,
        out_shape=[jax.ShapeDtypeStruct(*o) for o in out],
        in_specs=specs,
        out_specs=[place] * len(out),
        scratch_shapes=scratch,
        compiler_params=pltpu.CompilerParams(vmem_limit_bytes=14 * 1024 * 1024),
        cost_estimate=pl.CostEstimate(flops=flops, bytes_accessed=moved, transcendentals=0),
        name=name,
    )


def per_device(nz, nx, ny, x, g, w, lengths):
    rows, width = x.shape
    block = g.shape[1]
    half = block // 2
    features = ny * half
    lanes = 128
    work = 2 * rows * features * width
    group = (lax.axis_index("z") * nx + lax.axis_index("x")) * 2 + lax.axis_index("c")
    swap = [(0, 1), (1, 0)]

    place = group.astype(jnp.int32).reshape(1)
    (copies,) = call(sort_kernel, [((ny, rows, block), g.dtype)], [SMEM, VMEM], "sort", moved=2_000_000)(place, g)
    grads = lax.all_to_all(copies, "tensor", 0, 0)

    turned = ((features, rows), g.dtype)
    oth, own_g, oth_g, live_x = call(
        other_kernel,
        [((features, width), jnp.float32), turned, turned, (x.shape, x.dtype)],
        [SMEM, SMEM, VMEM, VMEM],
        "weight_grads_other",
        flops=work,
        moved=3_000_000,
    )(lengths, place, grads, x)
    got = lax.ppermute(oth, "c", swap)
    back = ((rows, features), g.dtype)
    mine, own_g, oth_g = call(
        own_kernel,
        [((features, width), jnp.float32), back, back],
        [SMEM, SMEM, VMEM, VMEM, VMEM],
        "weight_grads_own",
        flops=work,
        moved=3_000_000,
    )(lengths, place, own_g, oth_g, live_x)

    peers = nz * nx
    (code,) = call(functools.partial(pack_kernel, nx), [((peers, 8, 2 * width + lanes), jnp.int16)], [VMEM] * 3, "pack", moved=4_000_000)(
        mine.reshape(peers, 8, width), got.reshape(peers, 8, width), w
    )
    code = lax.all_to_all(code, ("x", "z"), 0, 0)
    (own_w,) = call(functools.partial(weights_kernel, nx), [((peers, 8, width), w.dtype)], [VMEM], "unpack_weights", moved=1_500_000)(code)
    own_w = own_w.reshape(features, width)
    oth_w = lax.ppermute(own_w, "c", swap)
    scale = 1.0 / math.sqrt(rows * peers * 2)
    (grad_weight,) = call(
        functools.partial(sum_kernel, scale), [((8, width), jnp.float32)], [VMEM], "unpack_sum", moved=1_000_000
    )(code)
    (part,) = call(
        first_kernel, [((rows, width), jnp.float32)], [VMEM] * 2, "input_grads_own", flops=work, moved=3_000_000
    )(own_g, own_w)
    (grad_input,) = call(
        input_kernel,
        [((rows, width), jnp.bfloat16)],
        [VMEM] * 3,
        "input_grads",
        scratch=[pltpu.VMEM((rows, width), w.dtype), pltpu.SemaphoreType.DMA((4,))],
        flops=work,
        moved=4_000_000,
        place=HBM,
    )(part, oth_g, oth_w)
    return (grad_input, grad_weight)


def solution(mesh):
    dp, ny = mesh.shape["dp"], mesh.shape["tensor"]
    nz, nx = ny, dp // (2 * ny)
    fine = Mesh(mesh.devices.reshape(nz, nx, 2, ny), ("z", "x", "c", "tensor"))
    both = P(("z", "x", "c"), "tensor")
    return jax.shard_map(
        functools.partial(per_device, nz, nx, ny),
        mesh=fine,
        in_specs=(both, both, both, P()),
        out_specs=(both, both),
        check_vma=False,
    )
```
